32 devices in a mesh: group: 2 (over y), row: 4 (over z), col: 2 (over x), depth: 2 (over core).
Axes of the slice: x: 2, y: 2, z: 4, core: 2. Of those that a mesh axis runs over, the one named last changes fastest.
Arguments:
- preact: bfloat16 [1024, 24576], P(('group', 'col', 'depth'), 'row'), parts along dimension 0, may hold values from -6 to 6
- weight: bfloat16 [24576, 6144], P('row', ('col', 'depth')), may hold values from -0.0390625 to 0.0390625
- out_grad: bfloat16 [1024, 6144], P(('group', 'row'), ('col', 'depth')), parts along dimension 0, may hold values from -6 to 6
Outputs:
- preact_grad: bfloat16 [1024, 24576], P(('group', 'col', 'depth'), 'row'), parts along dimension 0
- weight_grad: bfloat16 [49152, 6144], P(('group', 'row'), ('col', 'depth')), parts along dimension 0
The draws below stay inside these ranges and needn't reach their ends.
There are 2 independent parts, one for each index of `group`. The reference program is written for one: setup_inputs(seed, part) draws one part's arguments, and reference() takes and returns one part's arrays. A program takes and returns all parts, laid end to end along the dimension named above; an argument that names none is the same for every part. Nothing has to cross between parts.
All inputs are finite; a program needn't handle non-finite values.
Results may differ from the reference program's by a relative error of at most 0.0047.
Values may be sent and summed in bfloat16 or wider, within the bound.
No kernel may reach another device: no remote copies, remote signals or barrier semaphores. Data moves between devices by JAX's collectives and lax.ppermute only.
A program may use at most 256 MiB of HBM per device.

```python
import math
import jax
import jax.numpy as jnp

D = 6144
FF = 24576
TOKENS = 512


def block_scale(rng, dims, cuts, smallest, high):
    def one(dim, shards_of):
        steps = jax.random.uniform(jax.random.fold_in(jax.random.fold_in(rng, 6), dim), (shards_of,), jnp.float32, smallest / len(cuts), high / len(cuts))
        return jnp.repeat(jnp.exp(steps), dims[dim] // shards_of).reshape((-1,) + (1,) * (len(dims) - dim - 1))

    factor_of = one(*cuts[0])
    for cut in cuts[1:]:
        factor_of = factor_of * one(*cut)
    return factor_of


def normal_values(own_key, dims, width, reach, split=(), kind=jnp.bfloat16):
    array = width * jax.random.normal(own_key, dims, jnp.float32)
    if split:
        array = array * block_scale(own_key, dims, split, -0.22, 0.18)
    return jnp.clip(array, -reach, reach).astype(kind)


def setup_inputs(seed: int = 0, part: int = 0) -> dict:
    key_of = jax.random.split(jax.random.key(seed), 4)
    part_splits = jax.random.split(jax.random.fold_in(key_of[3], part), 4)
    preact = normal_values(part_splits[0], (TOKENS, FF), 1.5, 6.0, ((0, 4), (1, 4)))
    weight = normal_values(key_of[1], (FF, D), FF ** -0.5, 0.0390625, ((0, 4), (1, 4)))
    out_grad = normal_values(part_splits[2], (TOKENS, D), 1.0, 6.0, ((0, 4), (1, 4)))
    return {"preact": preact, "weight": weight, "out_grad": out_grad}


root_two_pi = 0.7978845608
cubic = 0.044715

def gelu_value(value):
    inner = jnp.tanh(root_two_pi * (value + cubic * value * value * value))
    return 0.5 * value * (1.0 + inner)

def gelu_slope(value):
    inner = jnp.tanh(root_two_pi * (value + cubic * value * value * value))
    return 0.5 * (1.0 + inner) + 0.5 * value * (1.0 - inner * inner) * root_two_pi * (1.0 + 3.0 * cubic * value * value)

def reference(preact, weight, out_grad):
    wide = preact.astype(jnp.float32)
    hidden = gelu_value(wide).astype(jnp.bfloat16)
    scale = 1.0 / math.sqrt(out_grad.shape[0])
    weight_grad = (jnp.dot(hidden.T, out_grad, preferred_element_type=jnp.float32) * scale).astype(jnp.bfloat16)
    hidden_grad = jnp.dot(out_grad, weight.T, preferred_element_type=jnp.float32)
    preact_grad = (hidden_grad * gelu_slope(wide)).astype(jnp.bfloat16)
    return (preact_grad, weight_grad)
```

```python
import math

import jax
import jax.numpy as jnp
from jax import lax
from jax.sharding import PartitionSpec as P

root_two_pi = 0.7978845608
cubic = 0.044715
f32 = jnp.float32
bf16 = jnp.bfloat16

HIDDEN_CHUNKS = 4
PARTIAL_CHUNKS = 4


def gelu_value(value):
    inner = jnp.tanh(root_two_pi * (value + cubic * value * value * value))
    return 0.5 * value * (1.0 + inner)


def gelu_slope(value):
    inner = jnp.tanh(root_two_pi * (value + cubic * value * value * value))
    return 0.5 * (1.0 + inner) + 0.5 * value * (1.0 - inner * inner) * root_two_pi * (
        1.0 + 3.0 * cubic * value * value
    )


def to_next(array, axis, size, hop):
    return lax.ppermute(array, axis, [(i, (i + hop) % size) for i in range(size)])


def from_next(array, axis, size, hop):
    return lax.ppermute(array, axis, [((i + hop) % size, i) for i in range(size)])


def solution(mesh):
    rows, cols, depths = mesh.shape["row"], mesh.shape["col"], mesh.shape["depth"]

    def row_blocks(out_grad):
        if rows > 4:
            whole = lax.all_gather(out_grad, "row", axis=0, tiled=False)
            own = lax.axis_index("row")
            return [
                lax.dynamic_index_in_dim(whole, lax.rem(own - s + rows, rows), 0, False)
                for s in range(rows)
            ]
        blocks = [out_grad]
        for _ in range(rows - 1):
            blocks.append(to_next(blocks[-1], "row", rows, 1))
        return blocks

    def per_device(preact, weight, out_grad):
        block, features = preact.shape
        row_tokens, width = out_grad.shape
        tokens = row_tokens * rows
        scale = 1.0 / math.sqrt(tokens)
        x, d, z = lax.axis_index("col"), lax.axis_index("depth"), lax.axis_index("row")

        stack = jnp.stack(row_blocks(out_grad))
        per_block = block // row_tokens
        ordered = []
        for dd in range(depths):
            for dx in range(cols):
                owner = lax.rem(x + dx, cols) * depths + lax.rem(d + dd, depths)
                for part in range(per_block):
                    place = lax.rem(z - (owner * per_block + part) + rows, rows)
                    ordered.append(lax.dynamic_index_in_dim(stack, place, 0, False))
        grads = jnp.concatenate(ordered, axis=0)
        half = cols * block

        wide = features // HIDDEN_CHUNKS
        hidden = []
        for c in range(HIDDEN_CHUNKS):
            own = gelu_value(preact[:, c * wide : (c + 1) * wide].astype(f32)).astype(bf16)
            mine = [own] + [from_next(own, "col", cols, dx) for dx in range(1, cols)]
            mine = jnp.concatenate(mine, axis=0)
            both = [mine] + [from_next(mine, "depth", depths, dd) for dd in range(1, depths)]
            hidden.append(jnp.concatenate(both, axis=0))

        wide = features // PARTIAL_CHUNKS
        pieces = []
        for c in range(PARTIAL_CHUNKS):
            rows_of = weight[c * wide : (c + 1) * wide]
            part = lax.dot_general(
                grads, rows_of, (((1,), (1,)), ((), ())), preferred_element_type=f32
            )
            total = part[:half]
            for dd in range(1, depths):
                sent = part[dd * half : (dd + 1) * half].astype(bf16)
                total = total + to_next(sent, "depth", depths, dd).astype(f32)
            mine = total[:block]
            for dx in range(1, cols):
                sent = total[dx * block : (dx + 1) * block].astype(bf16)
                mine = mine + to_next(sent, "col", cols, dx).astype(f32)
            value = preact[:, c * wide : (c + 1) * wide].astype(f32)
            pieces.append((mine * gelu_slope(value)).astype(bf16))
        preact_grad = jnp.concatenate(pieces, axis=1)

        weight_grad = []
        for part in hidden:
            summed = lax.dot_general(
                part, grads, (((0,), (0,)), ((), ())), preferred_element_type=f32
            )
            weight_grad.append((summed * scale).astype(bf16))
        return preact_grad, jnp.concatenate(weight_grad, axis=0)

    return jax.shard_map(
        per_device,
        mesh=mesh,
        in_specs=(
            P(("group", "col", "depth"), "row"),
            P("row", ("col", "depth")),
            P(("group", "row"), ("col", "depth")),
        ),
        out_specs=(P(("group", "col", "depth"), "row"), P(("group", "row"), ("col", "depth"))),
        check_vma=False,
    )
```

```python
import math

import jax
import jax.numpy as jnp
from jax import lax
from jax.experimental import pallas as pl
from jax.experimental.pallas import tpu as pltpu
from jax.sharding import PartitionSpec as P

root_two_pi = 0.7978845608
cubic = 0.044715
f32 = jnp.float32
bf16 = jnp.bfloat16

LANES = 128
WEIGHT_CUTS = (1, 1, 1, 1)
PARTIAL_CUTS = (1, 1, 1, 1)
TILE = 896
VMEM = 48 * 2**20
PARTIAL_COST = 0.01
WEIGHT_COST = 0.1
ANY = pl.BlockSpec(memory_space=pl.ANY)


def gelu_value(value):
    inner = jnp.tanh(root_two_pi * (value + cubic * value * value * value))
    return 0.5 * value * (1.0 + inner)


def gelu_slope(value):
    inner = jnp.tanh(root_two_pi * (value + cubic * value * value * value))
    return 0.5 * (1.0 + inner) + 0.5 * value * (1.0 - inner * inner) * root_two_pi * (
        1.0 + 3.0 * cubic * value * value
    )


def to_next(array, axis, size, hop):
    return lax.ppermute(array, axis, [(i, (i + hop) % size) for i in range(size)])


def from_next(array, axis, size, hop):
    return lax.ppermute(array, axis, [((i + hop) % size, i) for i in range(size)])


def cut(length, shares):
    total, units, done, low, chunks = sum(shares), length // LANES, 0, 0, []
    for share in shares:
        done += share
        high = units * done // total
        if high > low:
            chunks.append((low * LANES, (high - low) * LANES))
        low = high
    return chunks


def tile_of(offset, size, most=TILE):
    step = math.gcd(offset, size)
    best = LANES
    for tile in range(LANES, min(step, most) + 1, LANES):
        if step % tile == 0:
            best = tile
    return best


def call(kernel, name, grid, ins, in_specs, outs, out_specs, after=(), into=None, flops=0):
    extra = list(after) + ([] if into is None else [into])
    count = len(ins)

    def body(*refs):
        kernel(*refs[:count], *refs[count + len(extra) :])

    return pl.pallas_call(
        body,
        grid=grid,
        in_specs=list(in_specs) + [ANY] * len(extra),
        out_specs=list(out_specs),
        out_shape=list(outs),
        input_output_aliases={} if into is None else {count + len(extra) - 1: 0},
        cost_estimate=pl.CostEstimate(
            flops=flops,
            bytes_accessed=1024,
            transcendentals=0,
        ),
        compiler_params=pltpu.CompilerParams(vmem_limit_bytes=VMEM),
        name=name,
    )(*ins, *extra)


def columns(rows, tile, start=0):
    return pl.BlockSpec((rows, tile), lambda i: (0, start + i))


def fixed(shape):
    return pl.BlockSpec(shape, lambda i: (0,) * len(shape))


def split_rows(array, pieces, after):
    rows, width = array.shape[0] // pieces, array.shape[1]

    def kernel(array_ref, *piece_refs):
        for j, ref in enumerate(piece_refs):
            ref[...] = array_ref[j * rows : (j + 1) * rows]

    return call(
        kernel,
        "split_rows",
        (1,),
        [array],
        [fixed(array.shape)],
        [jax.ShapeDtypeStruct((rows, width), array.dtype)] * pieces,
        [fixed((rows, width))] * pieces,
        after,
    )


def hidden_part(preact, offset, size, after):
    block = preact.shape[0]
    tile = tile_of(offset, size)

    def kernel(preact_ref, hidden_ref):
        hidden_ref[...] = gelu_value(preact_ref[...].astype(f32)).astype(bf16)

    return call(
        kernel,
        "hidden_part",
        (size // tile,),
        [preact],
        [columns(block, tile, offset // tile)],
        [jax.ShapeDtypeStruct((block, size), bf16)],
        [columns(block, tile)],
        after,
    )[0]


def slopes(preact, after):
    block, features = preact.shape
    tile = tile_of(0, features)

    def kernel(preact_ref, slope_ref):
        slope_ref[...] = gelu_slope(preact_ref[...].astype(f32))

    return call(
        kernel,
        "slopes",
        (features // tile,),
        [preact],
        [columns(block, tile)],
        [jax.ShapeDtypeStruct((block, features), f32)],
        [columns(block, tile)],
        after,
    )[0]


def tokens_first(grads_ref, others, weight_ref, weights, half):
    dims = (((1,), (1,)), ((), ()))
    product = lax.dot_general(
        grads_ref[:half], weight_ref[...], dims, preferred_element_type=f32
    )
    for other, rows in zip(others, weights):
        product = product + lax.dot_general(
            other[...], rows[...], dims, preferred_element_type=f32
        )
    return product


def partial_products(grads, others, weight, weights, offset, size, block, after):
    half, width = others[0].shape if others else grads.shape
    tile = tile_of(offset, size)
    start = offset // tile
    count = len(others)

    def kernel(grads_ref, weight_ref, *refs):
        own_ref, send_ref = refs[-2:]
        product = tokens_first(grads_ref, refs[:count], weight_ref, refs[count:-2], half)
        own_ref[...] = product[:block]
        send_ref[...] = product[block:].astype(bf16)

    spec = pl.BlockSpec((tile, width), lambda i: (start + i, 0))
    return call(
        kernel,
        "partial_products",
        (size // tile,),
        [grads, weight, *others, *weights],
        [fixed((half, width)), spec] + [fixed((half, width))] * count + [spec] * count,
        [
            jax.ShapeDtypeStruct((block, size), f32),
            jax.ShapeDtypeStruct((half - block, size), bf16),
        ],
        [columns(block, tile), columns(half - block, tile)],
        after,
        flops=int(PARTIAL_COST * 2 * 2 * half * width * size),
    )


def first_products(pieces, other_pieces, place_of, weight, weights, size, block, half, tokens, after):
    tile = tile_of(0, size)
    rows, width = pieces[0][0].shape
    groups = [pieces] + other_pieces
    parts = [part for group in groups for piece in group for part in piece]
    split, entries, count = len(pieces), len(pieces[0]), len(other_pieces)
    held = rows * split

    def kernel(*refs):
        weight_ref, *refs_of = refs[len(parts) : len(parts) + 1 + count]
        outs = refs[len(parts) + 1 + count :]
        grads_ref, other_refs, own_ref, send_ref = outs[0], outs[1:-2], outs[-2], outs[-1]

        @pl.when(pl.program_id(0) == 0)
        def _():
            for j in range(split):
                for s in range(entries):
                    place = place_of(s)
                    at = pl.multiple_of(place * held + j * rows, rows)
                    grads_ref[pl.ds(at, rows)] = refs[j * entries + s][...]

                    @pl.when(place * held < half)
                    def _():
                        for k, other in enumerate(other_refs):
                            source = refs[((k + 1) * split + j) * entries + s]
                            other[pl.ds(at, rows)] = source[...]

        product = tokens_first(grads_ref, other_refs, weight_ref, refs_of, half)
        own_ref[...] = product[:block]
        send_ref[...] = product[block:].astype(bf16)

    spec = pl.BlockSpec((tile, width), lambda i: (i, 0))
    grads, *rest = call(
        kernel,
        "first_products",
        (size // tile,),
        parts + [weight, *weights],
        [fixed((rows, width))] * len(parts) + [spec] * (1 + count),
        [jax.ShapeDtypeStruct((tokens, width), bf16)]
        + [jax.ShapeDtypeStruct((half, width), bf16)] * count
        + [
            jax.ShapeDtypeStruct((block, size), f32),
            jax.ShapeDtypeStruct((half - block, size), bf16),
        ],
        [fixed((tokens, width))]
        + [fixed((half, width))] * count
        + [columns(block, tile), columns(half - block, tile)],
        after,
        flops=int(PARTIAL_COST * 2 * 2 * half * width * size),
    )
    return grads, rest[:-2], rest[-2], rest[-1]


def weight_products(blocks, grads, into, offset, size, scale, after):
    tokens, width = grads.shape
    block, features = blocks[0].shape
    tile = tile_of(offset, size)
    start = offset // tile

    def kernel(*refs):
        grads_ref, out_ref = refs[-2:]
        hidden = jnp.concatenate([ref[...] for ref in refs[:-2]], axis=0)
        product = lax.dot_general(
            hidden, grads_ref[...], (((0,), (0,)), ((), ())), preferred_element_type=f32
        )
        out_ref[...] = (product * scale).astype(bf16)

    return call(
        kernel,
        "weight_products",
        (size // tile,),
        blocks + [grads],
        [columns(block, tile, start)] * len(blocks) + [fixed((tokens, width))],
        [jax.ShapeDtypeStruct((features, width), bf16)],
        [pl.BlockSpec((tile, width), lambda i: (start + i, 0))],
        after,
        into,
        int(WEIGHT_COST * 2 * tokens * width * size),
    )[0]


def last_step(slope, keep, far, into, offset, after):
    block, features = slope.shape
    size = keep.shape[1]
    tile = tile_of(offset, size, size)
    terms = list(far)

    def kernel(slope_ref, keep_ref, *refs):
        total = keep_ref[...]
        for ref in refs[:-1]:
            total = total + ref[...].astype(f32)
        refs[-1][...] = (total * slope_ref[...]).astype(bf16)

    return call(
        kernel,
        "last_step",
        (size // tile,),
        [slope, keep] + terms,
        [columns(block, tile, offset // tile)] + [columns(block, tile)] * (1 + len(terms)),
        [jax.ShapeDtypeStruct((block, features), bf16)],
        [columns(block, tile, offset // tile)],
        after,
        into,
    )[0]


def solution(mesh):
    rows, cols, depths = mesh.shape["row"], mesh.shape["col"], mesh.shape["depth"]

    def per_device(preact, weight, out_grad):
        block, features = preact.shape
        row_tokens, width = out_grad.shape
        tokens = row_tokens * rows
        scale = 1.0 / math.sqrt(tokens)
        half = cols * block
        per_block = block // row_tokens
        ring = rows <= 4

        hidden = [hidden_part(preact, 0, features, [])]
        parts = split_rows(out_grad, 2 if ring else 1, [hidden[0]])
        hidden += [from_next(hidden[0], "col", cols, dx) for dx in range(1, cols)]
        slope = slopes(preact, [hidden[0]])

        if ring:
            pieces = [[part] for part in parts]
            for hop in range(rows - 1):
                for piece in pieces:
                    piece.append(to_next(piece[-1], "row", rows, 1))
                if hop == 0:
                    pieces[-1][-1], slope = lax.optimization_barrier((pieces[-1][-1], slope))
        else:
            whole = lax.all_gather(parts[0], "row", axis=0, tiled=False)
            z = lax.axis_index("row")
            pieces = [
                [
                    lax.dynamic_index_in_dim(whole, lax.rem(z - s + rows, rows), 0, False)
                    for s in range(rows)
                ]
            ]

        def place_of(s):
            row = lax.rem(lax.axis_index("row") - s + rows, rows)
            owner = row // per_block
            dx = lax.rem(owner // depths - lax.axis_index("col") + cols, cols)
            dd = lax.rem(lax.rem(owner, depths) - lax.axis_index("depth") + depths, depths)
            return (dd * cols + dx) * per_block + lax.rem(row, per_block)

        hops = range(1, depths)
        weights = [from_next(weight, "depth", depths, dd) for dd in hops]
        if ring:
            for piece in pieces:
                *piece[:-1], _ = lax.optimization_barrier((*piece[:-1], pieces[-1][-2]))
        other_pieces = [
            [[from_next(part, "depth", depths, dd) for part in piece] for piece in pieces]
            for dd in hops
        ]

        chunks = cut(features, PARTIAL_CUTS)
        count = len(chunks)
        owns, far = [], []
        for c, (offset, size) in enumerate(chunks):
            if c == 0:
                grads, others, own, send = first_products(
                    pieces, other_pieces, place_of, weight, weights, size, block, half, tokens,
                    [slope],
                )
            else:
                own, send = partial_products(
                    grads, others, weight, weights, offset, size, block, owns[-1:]
                )
            owns.append(own)
            far.append(
                [
                    to_next(send[(dx - 1) * block : dx * block], "col", cols, dx)
                    for dx in range(1, cols)
                ]
            )

        *blocks, _ = lax.optimization_barrier((*hidden, owns[min(1, count - 1)]))
        blocks += [from_next(part, "depth", depths, dd) for dd in hops for part in blocks]
        weight_grad = None
        for k, (offset, size) in enumerate(cut(features, WEIGHT_CUTS)):
            after = owns[-1:] if k == 0 else far[k - 1][-1:] if k < count else []
            weight_grad = weight_products(blocks, grads, weight_grad, offset, size, scale, after)
        preact_grad = None
        for c in range(count):
            preact_grad = last_step(
                slope, owns[c], far[c], preact_grad, chunks[c][0], [weight_grad] if c == 0 else []
            )
        return preact_grad, weight_grad

    return jax.shard_map(
        per_device,
        mesh=mesh,
        in_specs=(
            P(("group", "col", "depth"), "row"),
            P("row", ("col", "depth")),
            P(("group", "row"), ("col", "depth")),
        ),
        out_specs=(P(("group", "col", "depth"), "row"), P(("group", "row"), ("col", "depth"))),
        check_vma=False,
    )
```

```python
import math

import jax
import jax.numpy as jnp
from jax import lax
from jax.experimental import pallas as pl
from jax.experimental.pallas import tpu as pltpu
from jax.sharding import PartitionSpec as P

root_two_pi = 0.7978845608
cubic = 0.044715
f32 = jnp.float32
bf16 = jnp.bfloat16

LANES = 128
WEIGHT_CUTS = (1,)
PARTIAL_CUTS = (1, 1, 1, 1)
TILE = 896
VMEM = 40 * 2**20
PARTIAL_COST = 0.01
LAST_COST = 0.1
ANY = pl.BlockSpec(memory_space=pl.ANY)


def gelu_value(value):
    inner = jnp.tanh(root_two_pi * (value + cubic * value * value * value))
    return 0.5 * value * (1.0 + inner)


def gelu_slope(value):
    inner = jnp.tanh(root_two_pi * (value + cubic * value * value * value))
    return 0.5 * (1.0 + inner) + 0.5 * value * (1.0 - inner * inner) * root_two_pi * (
        1.0 + 3.0 * cubic * value * value
    )


def to_next(array, axis, size, hop):
    return lax.ppermute(array, axis, [(i, (i + hop) % size) for i in range(size)])


def from_next(array, axis, size, hop):
    return lax.ppermute(array, axis, [((i + hop) % size, i) for i in range(size)])


def cut(length, shares):
    total, units, done, low, chunks = sum(shares), length // LANES, 0, 0, []
    for share in shares:
        done += share
        high = units * done // total
        if high > low:
            chunks.append((low * LANES, (high - low) * LANES))
        low = high
    return chunks


def tile_of(offset, size, most=TILE):
    step = math.gcd(offset, size)
    best = LANES
    for tile in range(LANES, min(step, most) + 1, LANES):
        if step % tile == 0:
            best = tile
    return best


def call(kernel, name, grid, ins, in_specs, outs, out_specs, after=(), into=None, flops=0):
    extra = list(after) + ([] if into is None else [into])
    count = len(ins)

    def body(*refs):
        kernel(*refs[:count], *refs[count + len(extra) :])

    return pl.pallas_call(
        body,
        grid=grid,
        in_specs=list(in_specs) + [ANY] * len(extra),
        out_specs=list(out_specs),
        out_shape=list(outs),
        input_output_aliases={} if into is None else {count + len(extra) - 1: 0},
        cost_estimate=pl.CostEstimate(
            flops=flops,
            bytes_accessed=1024,
            transcendentals=0,
        ),
        compiler_params=pltpu.CompilerParams(vmem_limit_bytes=VMEM),
        name=name,
    )(*ins, *extra)


def columns(rows, tile, start=0):
    return pl.BlockSpec((rows, tile), lambda i: (0, start + i))


def fixed(shape):
    return pl.BlockSpec(shape, lambda i: (0,) * len(shape))


def split_rows(array, pieces, after):
    rows, width = array.shape[0] // pieces, array.shape[1]

    def kernel(array_ref, *piece_refs):
        for j, ref in enumerate(piece_refs):
            ref[...] = array_ref[j * rows : (j + 1) * rows]

    return call(
        kernel,
        "split_rows",
        (1,),
        [array],
        [fixed(array.shape)],
        [jax.ShapeDtypeStruct((rows, width), array.dtype)] * pieces,
        [fixed((rows, width))] * pieces,
        after,
    )


def hidden_part(preact, offset, size, after):
    block = preact.shape[0]
    tile = tile_of(offset, size)

    def kernel(preact_ref, hidden_ref):
        hidden_ref[...] = gelu_value(preact_ref[...].astype(f32)).astype(bf16)

    return call(
        kernel,
        "hidden_part",
        (size // tile,),
        [preact],
        [columns(block, tile, offset // tile)],
        [jax.ShapeDtypeStruct((block, size), bf16)],
        [columns(block, tile)],
        after,
    )[0]


def slopes(preact, after):
    block, features = preact.shape
    tile = tile_of(0, features)

    def kernel(preact_ref, slope_ref):
        slope_ref[...] = gelu_slope(preact_ref[...].astype(f32))

    return call(
        kernel,
        "slopes",
        (features // tile,),
        [preact],
        [columns(block, tile)],
        [jax.ShapeDtypeStruct((block, features), f32)],
        [columns(block, tile)],
        after,
    )[0]


def in_order(pieces, place_of, half, tokens):
    rows, width = pieces[0][0].shape
    parts = [part for piece in pieces for part in piece]
    entries, held = len(pieces[0]), rows * len(pieces)

    def kernel(*refs):
        first_ref, second_ref = refs[-2:]
        for j in range(len(pieces)):
            for s in range(entries):
                part, row = refs[j * entries + s], place_of(s) * held

                @pl.when(row < half)
                def _():
                    first_ref[pl.ds(pl.multiple_of(row + j * rows, rows), rows)] = part[...]

                @pl.when(row >= half)
                def _():
                    at = pl.multiple_of(row - half + j * rows, rows)
                    second_ref[pl.ds(at, rows)] = part[...]

    shapes = [(half, width), (tokens - half, width)]
    return call(
        kernel,
        "in_order",
        (1,),
        parts,
        [fixed((rows, width))] * len(parts),
        [jax.ShapeDtypeStruct(shape, bf16) for shape in shapes],
        [fixed(shape) for shape in shapes],
    )


def partial_products(grads, weights, offset, size, block, after):
    half, width = grads[0].shape
    tile = tile_of(offset, size)
    start = offset // tile
    count = len(grads)

    def kernel(*refs):
        own_ref, send_ref = refs[-2:]
        product = 0.0
        for part, rows in zip(refs[:count], refs[count:-2]):
            product = product + lax.dot_general(
                part[...], rows[...], (((1,), (1,)), ((), ())), preferred_element_type=f32
            )
        own_ref[...] = product[:block]
        send_ref[...] = product[block:].astype(bf16)

    return call(
        kernel,
        "partial_products",
        (size // tile,),
        [*grads, *weights],
        [fixed((half, width))] * count
        + [pl.BlockSpec((tile, width), lambda i: (start + i, 0))] * count,
        [
            jax.ShapeDtypeStruct((block, size), f32),
            jax.ShapeDtypeStruct((half - block, size), bf16),
        ],
        [columns(block, tile), columns(half - block, tile)],
        after,
        flops=int(PARTIAL_COST * 2 * 2 * half * width * size),
    )


def weight_products(blocks, grads, into, offset, size, scale, after):
    width = grads[0].shape[1]
    block, features = blocks[0].shape
    count = len(blocks)
    tile = tile_of(offset, size)
    start = offset // tile

    def kernel(*refs):
        out_ref = refs[-1]
        hidden = jnp.concatenate([ref[...] for ref in refs[:count]], axis=0)
        rows = jnp.concatenate([ref[...] for ref in refs[count:-1]], axis=0)
        product = lax.dot_general(
            hidden, rows, (((0,), (0,)), ((), ())), preferred_element_type=f32
        )
        out_ref[...] = (product * scale).astype(bf16)

    return call(
        kernel,
        "weight_products",
        (size // tile,),
        [*blocks, *grads],
        [columns(block, tile, start)] * count + [fixed(part.shape) for part in grads],
        [jax.ShapeDtypeStruct((features, width), bf16)],
        [pl.BlockSpec((tile, width), lambda i: (start + i, 0))],
        after,
        into,
        1024,
    )[0]


def last_step(slope, keep, far, into, offset, after):
    block, features = slope.shape
    size = keep.shape[1]
    tile = tile_of(offset, size, size)
    terms = list(far)

    def kernel(slope_ref, keep_ref, *refs):
        total = keep_ref[...]
        for ref in refs[:-1]:
            total = total + ref[...].astype(f32)
        refs[-1][...] = (total * slope_ref[...]).astype(bf16)

    return call(
        kernel,
        "last_step",
        (size // tile,),
        [slope, keep] + terms,
        [columns(block, tile, offset // tile)] + [columns(block, tile)] * (1 + len(terms)),
        [jax.ShapeDtypeStruct((block, features), bf16)],
        [columns(block, tile, offset // tile)],
        after,
        into,
        int(LAST_COST * 2**20 * size),
    )[0]


def solution(mesh):
    rows, cols, depths = mesh.shape["row"], mesh.shape["col"], mesh.shape["depth"]

    def per_device(preact, weight, out_grad):
        block, features = preact.shape
        row_tokens, width = out_grad.shape
        tokens = row_tokens * rows
        scale = 1.0 / math.sqrt(tokens)
        half = cols * block
        per_block = block // row_tokens
        ring = rows <= 4

        hidden = [hidden_part(preact, 0, features, [])]
        parts = split_rows(out_grad, 2 if ring else 1, [])
        hidden += [from_next(hidden[0], "col", cols, dx) for dx in range(1, cols)]
        slope = slopes(preact, [hidden[0]])

        if ring:
            pieces = [[part] for part in parts]
            for hop in range(rows - 1):
                for piece in pieces:
                    piece.append(to_next(piece[-1], "row", rows, 1))
        else:
            whole = lax.all_gather(parts[0], "row", axis=0, tiled=False)
            z = lax.axis_index("row")
            pieces = [
                [
                    lax.dynamic_index_in_dim(whole, lax.rem(z - s + rows, rows), 0, False)
                    for s in range(rows)
                ]
            ]

        def place_of(s):
            row = lax.rem(lax.axis_index("row") - s + rows, rows)
            owner = row // per_block
            dx = lax.rem(owner // depths - lax.axis_index("col") + cols, cols)
            dd = lax.rem(lax.rem(owner, depths) - lax.axis_index("depth") + depths, depths)
            return (dd * cols + dx) * per_block + lax.rem(row, per_block)

        hops = range(1, depths)
        first, second = in_order(pieces, place_of, half, tokens)
        weights = [weight] + [from_next(weight, "depth", depths, dd) for dd in hops]
        grads = [first] + [
            to_next(second[(dd - 1) * half : dd * half], "depth", depths, dd) for dd in hops
        ]

        chunks = cut(features, PARTIAL_CUTS)
        count = len(chunks)
        owns, far = [], []
        for c, (offset, size) in enumerate(chunks):
            after = owns[-1:] if owns else [slope]
            own, send = partial_products(grads, weights, offset, size, block, after)
            owns.append(own)
            far.append(
                [
                    to_next(send[(dx - 1) * block : dx * block], "col", cols, dx)
                    for dx in range(1, cols)
                ]
            )

        *blocks, _ = lax.optimization_barrier((*hidden, owns[0]))
        blocks += [from_next(part, "depth", depths, dd) for dd in hops for part in blocks]
        weight_grad = None
        for k, (offset, size) in enumerate(cut(features, WEIGHT_CUTS)):
            after = owns[-1:] if k == 0 else far[k - 1][-1:]
            weight_grad = weight_products(
                blocks, [first, second], weight_grad, offset, size, scale, after
            )
        preact_grad = None
        for c in range(count):
            preact_grad = last_step(
                slope, owns[c], far[c], preact_grad, chunks[c][0], [weight_grad] if c == 0 else []
            )
        return preact_grad, weight_grad

    return jax.shard_map(
        per_device,
        mesh=mesh,
        in_specs=(
            P(("group", "col", "depth"), "row"),
            P("row", ("col", "depth")),
            P(("group", "row"), ("col", "depth")),
        ),
        out_specs=(P(("group", "col", "depth"), "row"), P(("group", "row"), ("col", "depth"))),
        check_vma=False,
    )
```

```python
import math

import jax
import jax.numpy as jnp
from jax import lax
from jax.experimental import pallas as pl
from jax.experimental.pallas import tpu as pltpu
from jax.sharding import PartitionSpec as P

root_two_pi = 0.7978845608
cubic = 0.044715
f32 = jnp.float32
bf16 = jnp.bfloat16

LANES = 128
WEIGHT_CUTS = (1,)
PARTIAL_CUTS = (1, 1, 1, 1)
TILE = 896
VMEM = 40 * 2**20
PARTIAL_COST = 0.01
LAST_COST = 0.1
ANY = pl.BlockSpec(memory_space=pl.ANY)


def gelu_value(value):
    inner = jnp.tanh(root_two_pi * (value + cubic * value * value * value))
    return 0.5 * value * (1.0 + inner)


def gelu_slope(value):
    inner = jnp.tanh(root_two_pi * (value + cubic * value * value * value))
    return 0.5 * (1.0 + inner) + 0.5 * value * (1.0 - inner * inner) * root_two_pi * (
        1.0 + 3.0 * cubic * value * value
    )


def to_next(array, axis, size, hop):
    return lax.ppermute(array, axis, [(i, (i + hop) % size) for i in range(size)])


def from_next(array, axis, size, hop):
    return lax.ppermute(array, axis, [((i + hop) % size, i) for i in range(size)])


def cut(length, shares):
    total, units, done, low, chunks = sum(shares), length // LANES, 0, 0, []
    for share in shares:
        done += share
        high = units * done // total
        if high > low:
            chunks.append((low * LANES, (high - low) * LANES))
        low = high
    return chunks


def tile_of(offset, size, most=TILE):
    step = math.gcd(offset, size)
    best = LANES
    for tile in range(LANES, min(step, most) + 1, LANES):
        if step % tile == 0:
            best = tile
    return best


def call(kernel, name, grid, ins, in_specs, outs, out_specs, after=(), into=None, flops=0):
    extra = list(after) + ([] if into is None else [into])
    count = len(ins)

    def body(*refs):
        kernel(*refs[:count], *refs[count + len(extra) :])

    return pl.pallas_call(
        body,
        grid=grid,
        in_specs=list(in_specs) + [ANY] * len(extra),
        out_specs=list(out_specs),
        out_shape=list(outs),
        input_output_aliases={} if into is None else {count + len(extra) - 1: 0},
        cost_estimate=pl.CostEstimate(
            flops=flops,
            bytes_accessed=1024,
            transcendentals=0,
        ),
        compiler_params=pltpu.CompilerParams(vmem_limit_bytes=VMEM),
        name=name,
    )(*ins, *extra)


def columns(rows, tile, start=0):
    return pl.BlockSpec((rows, tile), lambda i: (0, start + i))


def fixed(shape):
    return pl.BlockSpec(shape, lambda i: (0,) * len(shape))


def split_rows(array, pieces, after):
    rows, width = array.shape[0] // pieces, array.shape[1]

    def kernel(array_ref, *piece_refs):
        for j, ref in enumerate(piece_refs):
            ref[...] = array_ref[j * rows : (j + 1) * rows]

    return call(
        kernel,
        "split_rows",
        (1,),
        [array],
        [fixed(array.shape)],
        [jax.ShapeDtypeStruct((rows, width), array.dtype)] * pieces,
        [fixed((rows, width))] * pieces,
        after,
    )


def hidden_part(preact, offset, size, after):
    block = preact.shape[0]
    tile = tile_of(offset, size)

    def kernel(preact_ref, hidden_ref):
        hidden_ref[...] = gelu_value(preact_ref[...].astype(f32)).astype(bf16)

    return call(
        kernel,
        "hidden_part",
        (size // tile,),
        [preact],
        [columns(block, tile, offset // tile)],
        [jax.ShapeDtypeStruct((block, size), bf16)],
        [columns(block, tile)],
        after,
    )[0]


def slopes(preact, after):
    block, features = preact.shape
    tile = tile_of(0, features)

    def kernel(preact_ref, slope_ref):
        slope_ref[...] = gelu_slope(preact_ref[...].astype(f32))

    return call(
        kernel,
        "slopes",
        (features // tile,),
        [preact],
        [columns(block, tile)],
        [jax.ShapeDtypeStruct((block, features), f32)],
        [columns(block, tile)],
        after,
    )[0]


def in_order(pieces, place_of, half, tokens, after):
    rows, width = pieces[0][0].shape
    parts = [part for piece in pieces for part in piece]
    entries, held = len(pieces[0]), rows * len(pieces)

    def kernel(*refs):
        first_ref, second_ref = refs[-2:]
        for j in range(len(pieces)):
            for s in range(entries):
                part, row = refs[j * entries + s], place_of(s) * held

                @pl.when(row < half)
                def _():
                    first_ref[pl.ds(pl.multiple_of(row + j * rows, rows), rows)] = part[...]

                @pl.when(row >= half)
                def _():
                    at = pl.multiple_of(row - half + j * rows, rows)
                    second_ref[pl.ds(at, rows)] = part[...]

    shapes = [(half, width), (tokens - half, width)]
    return call(
        kernel,
        "in_order",
        (1,),
        parts,
        [fixed((rows, width))] * len(parts),
        [jax.ShapeDtypeStruct(shape, bf16) for shape in shapes],
        [fixed(shape) for shape in shapes],
        after,
    )


def partial_products(grads, weights, offset, size, block, after):
    half, width = grads[0].shape
    tile = tile_of(offset, size)
    start = offset // tile
    count = len(grads)

    def kernel(*refs):
        own_ref, send_ref = refs[-2:]
        product = 0.0
        for part, rows in zip(refs[:count], refs[count:-2]):
            product = product + lax.dot_general(
                part[...], rows[...], (((1,), (1,)), ((), ())), preferred_element_type=f32
            )
        own_ref[...] = product[:block]
        send_ref[...] = product[block:].astype(bf16)

    return call(
        kernel,
        "partial_products",
        (size // tile,),
        [*grads, *weights],
        [fixed((half, width))] * count
        + [pl.BlockSpec((tile, width), lambda i: (start + i, 0))] * count,
        [
            jax.ShapeDtypeStruct((block, size), f32),
            jax.ShapeDtypeStruct((half - block, size), bf16),
        ],
        [columns(block, tile), columns(half - block, tile)],
        after,
        flops=int(PARTIAL_COST * 2 * 2 * half * width * size),
    )


def weight_products(blocks, cols, grads, into, offset, size, scale, after):
    width = grads[0].shape[1]
    block, features = blocks[0].shape
    count = len(blocks)
    tile = tile_of(offset, size)
    start = offset // tile

    def kernel(*refs):
        out_ref = refs[-1]
        hidden = [ref[...] for ref in refs[:count]]
        for k in range(count):
            if k % cols:
                hidden[k] = gelu_value(hidden[k].astype(f32)).astype(bf16)
        hidden = jnp.concatenate(hidden, axis=0)
        rows = jnp.concatenate([ref[...] for ref in refs[count:-1]], axis=0)
        product = lax.dot_general(
            hidden, rows, (((0,), (0,)), ((), ())), preferred_element_type=f32
        )
        out_ref[...] = (product * scale).astype(bf16)

    return call(
        kernel,
        "weight_products",
        (size // tile,),
        [*blocks, *grads],
        [columns(block, tile, start)] * count + [fixed(part.shape) for part in grads],
        [jax.ShapeDtypeStruct((features, width), bf16)],
        [pl.BlockSpec((tile, width), lambda i: (start + i, 0))],
        after,
        into,
        1024,
    )[0]


def last_step(slope, keep, far, into, offset, after):
    block, features = slope.shape
    size = keep.shape[1]
    tile = tile_of(offset, size, size)
    terms = list(far)

    def kernel(slope_ref, keep_ref, *refs):
        total = keep_ref[...]
        for ref in refs[:-1]:
            total = total + ref[...].astype(f32)
        refs[-1][...] = (total * slope_ref[...]).astype(bf16)

    return call(
        kernel,
        "last_step",
        (size // tile,),
        [slope, keep] + terms,
        [columns(block, tile, offset // tile)] + [columns(block, tile)] * (1 + len(terms)),
        [jax.ShapeDtypeStruct((block, features), bf16)],
        [columns(block, tile, offset // tile)],
        after,
        into,
        int(LAST_COST * 2**20 * size),
    )[0]


def solution(mesh):
    rows, cols, depths = mesh.shape["row"], mesh.shape["col"], mesh.shape["depth"]

    def per_device(preact, weight, out_grad):
        block, features = preact.shape
        row_tokens, width = out_grad.shape
        tokens = row_tokens * rows
        scale = 1.0 / math.sqrt(tokens)
        half = cols * block
        per_block = block // row_tokens
        ring = rows <= 4

        arrived = [from_next(preact, "col", cols, dx) for dx in range(1, cols)]
        parts = split_rows(out_grad, 2 if ring else 1, [])
        hidden = [hidden_part(preact, 0, features, [parts[0]])]
        slope = slopes(preact, [hidden[0]])

        if ring:
            pieces = [[part] for part in parts]
            for hop in range(rows - 1):
                for piece in pieces:
                    piece.append(to_next(piece[-1], "row", rows, 1))
        else:
            whole = lax.all_gather(parts[0], "row", axis=0, tiled=False)
            z = lax.axis_index("row")
            pieces = [
                [
                    lax.dynamic_index_in_dim(whole, lax.rem(z - s + rows, rows), 0, False)
                    for s in range(rows)
                ]
            ]

        def place_of(s):
            row = lax.rem(lax.axis_index("row") - s + rows, rows)
            owner = row // per_block
            dx = lax.rem(owner // depths - lax.axis_index("col") + cols, cols)
            dd = lax.rem(lax.rem(owner, depths) - lax.axis_index("depth") + depths, depths)
            return (dd * cols + dx) * per_block + lax.rem(row, per_block)

        hops = range(1, depths)
        first, second = in_order(pieces, place_of, half, tokens, [slope])
        weights = [weight] + [from_next(weight, "depth", depths, dd) for dd in hops]
        grads = [first] + [
            to_next(second[(dd - 1) * half : dd * half], "depth", depths, dd) for dd in hops
        ]

        chunks = cut(features, PARTIAL_CUTS)
        count = len(chunks)
        owns, far = [], []
        for c, (offset, size) in enumerate(chunks):
            after = owns[-1:]
            own, send = partial_products(grads, weights, offset, size, block, after)
            owns.append(own)
            far.append(
                [
                    to_next(send[(dx - 1) * block : dx * block], "col", cols, dx)
                    for dx in range(1, cols)
                ]
            )

        *raw, _ = lax.optimization_barrier((*arrived, owns[0]))
        blocks = hidden + raw
        blocks += [from_next(part, "depth", depths, dd) for dd in hops for part in blocks]
        weight_grad = None
        for k, (offset, size) in enumerate(cut(features, WEIGHT_CUTS)):
            after = owns[-1:] if k == 0 else far[k - 1][-1:]
            weight_grad = weight_products(
                blocks, cols, [first, second], weight_grad, offset, size, scale, after
            )
        preact_grad = None
        for c in range(count):
            preact_grad = last_step(
                slope, owns[c], far[c], preact_grad, chunks[c][0], [weight_grad] if c == 0 else []
            )
        return preact_grad, weight_grad

    return jax.shard_map(
        per_device,
        mesh=mesh,
        in_specs=(
            P(("group", "col", "depth"), "row"),
            P("row", ("col", "depth")),
            P(("group", "row"), ("col", "depth")),
        ),
        out_specs=(P(("group", "col", "depth"), "row"), P(("group", "row"), ("col", "depth"))),
        check_vma=False,
    )
```

```python
import math

import jax
import jax.numpy as jnp
from jax import lax
from jax.experimental import pallas as pl
from jax.experimental.pallas import tpu as pltpu
from jax.sharding import PartitionSpec as P

root_two_pi = 0.7978845608
cubic = 0.044715
f32 = jnp.float32
bf16 = jnp.bfloat16

LANES = 128
WEIGHT_CUTS = (1,)
PARTIAL_CUTS = (1, 1, 1, 1)
TILE = 896
VMEM = 40 * 2**20
PARTIAL_COST = 0.01
LAST_COST = 0.1
ANY = pl.BlockSpec(memory_space=pl.ANY)


def gelu_value(value):
    inner = jnp.tanh(root_two_pi * (value + cubic * value * value * value))
    return 0.5 * value * (1.0 + inner)


def gelu_slope(value):
    inner = jnp.tanh(root_two_pi * (value + cubic * value * value * value))
    return 0.5 * (1.0 + inner) + 0.5 * value * (1.0 - inner * inner) * root_two_pi * (
        1.0 + 3.0 * cubic * value * value
    )


def to_next(array, axis, size, hop):
    return lax.ppermute(array, axis, [(i, (i + hop) % size) for i in range(size)])


def from_next(array, axis, size, hop):
    return lax.ppermute(array, axis, [((i + hop) % size, i) for i in range(size)])


def cut(length, shares):
    total, units, done, low, chunks = sum(shares), length // LANES, 0, 0, []
    for share in shares:
        done += share
        high = units * done // total
        if high > low:
            chunks.append((low * LANES, (high - low) * LANES))
        low = high
    return chunks


def tile_of(offset, size, most=TILE):
    step = math.gcd(offset, size)
    best = LANES
    for tile in range(LANES, min(step, most) + 1, LANES):
        if step % tile == 0:
            best = tile
    return best


def call(kernel, name, grid, ins, in_specs, outs, out_specs, after=(), into=None, flops=0):
    extra = list(after) + ([] if into is None else [into])
    count = len(ins)

    def body(*refs):
        kernel(*refs[:count], *refs[count + len(extra) :])

    return pl.pallas_call(
        body,
        grid=grid,
        in_specs=list(in_specs) + [ANY] * len(extra),
        out_specs=list(out_specs),
        out_shape=list(outs),
        input_output_aliases={} if into is None else {count + len(extra) - 1: 0},
        cost_estimate=pl.CostEstimate(
            flops=flops,
            bytes_accessed=1024,
            transcendentals=0,
        ),
        compiler_params=pltpu.CompilerParams(vmem_limit_bytes=VMEM),
        name=name,
    )(*ins, *extra)


def columns(rows, tile, start=0):
    return pl.BlockSpec((rows, tile), lambda i: (0, start + i))


def fixed(shape):
    return pl.BlockSpec(shape, lambda i: (0,) * len(shape))


def split_rows(array, pieces, after):
    rows, width = array.shape[0] // pieces, array.shape[1]

    def kernel(array_ref, *piece_refs):
        for j, ref in enumerate(piece_refs):
            ref[...] = array_ref[j * rows : (j + 1) * rows]

    return call(
        kernel,
        "split_rows",
        (1,),
        [array],
        [fixed(array.shape)],
        [jax.ShapeDtypeStruct((rows, width), array.dtype)] * pieces,
        [fixed((rows, width))] * pieces,
        after,
    )


def hidden_part(preact, offset, size, after):
    block = preact.shape[0]
    tile = tile_of(offset, size)

    def kernel(preact_ref, hidden_ref):
        hidden_ref[...] = gelu_value(preact_ref[...].astype(f32)).astype(bf16)

    return call(
        kernel,
        "hidden_part",
        (size // tile,),
        [preact],
        [columns(block, tile, offset // tile)],
        [jax.ShapeDtypeStruct((block, size), bf16)],
        [columns(block, tile)],
        after,
    )[0]


def slopes(preact, after):
    block, features = preact.shape
    tile = tile_of(0, features)

    def kernel(preact_ref, slope_ref):
        slope_ref[...] = gelu_slope(preact_ref[...].astype(f32))

    return call(
        kernel,
        "slopes",
        (features // tile,),
        [preact],
        [columns(block, tile)],
        [jax.ShapeDtypeStruct((block, features), f32)],
        [columns(block, tile)],
        after,
    )[0]


def in_order(pieces, place_of, half, tokens, after):
    rows, width = pieces[0][0].shape
    parts = [part for piece in pieces for part in piece]
    entries, held = len(pieces[0]), rows * len(pieces)

    def kernel(*refs):
        first_ref, second_ref = refs[-2:]
        for j in range(len(pieces)):
            for s in range(entries):
                part, row = refs[j * entries + s], place_of(s) * held

                @pl.when(row < half)
                def _():
                    first_ref[pl.ds(pl.multiple_of(row + j * rows, rows), rows)] = part[...]

                @pl.when(row >= half)
                def _():
                    at = pl.multiple_of(row - half + j * rows, rows)
                    second_ref[pl.ds(at, rows)] = part[...]

    shapes = [(half, width), (tokens - half, width)]
    return call(
        kernel,
        "in_order",
        (1,),
        parts,
        [fixed((rows, width))] * len(parts),
        [jax.ShapeDtypeStruct(shape, bf16) for shape in shapes],
        [fixed(shape) for shape in shapes],
        after,
    )


def staged(weight, size, after):
    width = weight.shape[1]
    tile = tile_of(0, size)

    def kernel(weight_ref, copy_ref):
        copy_ref[...] = weight_ref[...]

    spec = pl.BlockSpec((tile, width), lambda i: (i, 0))
    return call(
        kernel,
        "staged",
        (size // tile,),
        [weight],
        [spec],
        [jax.ShapeDtypeStruct((size, width), bf16)],
        [spec],
        after,
    )[0]


def partial_products(grads, weights, offset, size, block, after, held=None):
    half, width = grads[0].shape
    tile = tile_of(offset, size)
    start = offset // tile
    count = len(grads)

    def kernel(*refs):
        own_ref, send_ref = refs[-2:]
        product = 0.0
        here = pl.ds(pl.multiple_of(pl.program_id(0) * tile, tile), tile)
        for k, (part, rows) in enumerate(zip(refs[:count], refs[count:-2])):
            rows_of = rows[here] if k == 0 and held is not None else rows[...]
            product = product + lax.dot_general(
                part[...], rows_of, (((1,), (1,)), ((), ())), preferred_element_type=f32
            )
        own_ref[...] = product[:block]
        send_ref[...] = product[block:].astype(bf16)

    spec = pl.BlockSpec((tile, width), lambda i: (start + i, 0))
    return call(
        kernel,
        "partial_products",
        (size // tile,),
        [*grads, *(weights if held is None else [held, *weights[1:]])],
        [fixed((half, width))] * count
        + [spec if held is None else fixed((size, width))]
        + [spec] * (count - 1),
        [
            jax.ShapeDtypeStruct((block, size), f32),
            jax.ShapeDtypeStruct((half - block, size), bf16),
        ],
        [columns(block, tile), columns(half - block, tile)],
        after,
        flops=int(PARTIAL_COST * 2 * 2 * half * width * size),
    )


def weight_products(blocks, cols, grads, into, offset, size, scale, after):
    width = grads[0].shape[1]
    block, features = blocks[0].shape
    count = len(blocks)
    tile = tile_of(offset, size)
    start = offset // tile

    def kernel(*refs):
        out_ref = refs[-1]
        hidden = [ref[...] for ref in refs[:count]]
        for k in range(count):
            if k % cols:
                hidden[k] = gelu_value(hidden[k].astype(f32)).astype(bf16)
        hidden = jnp.concatenate(hidden, axis=0)
        rows = jnp.concatenate([ref[...] for ref in refs[count:-1]], axis=0)
        product = lax.dot_general(
            hidden, rows, (((0,), (0,)), ((), ())), preferred_element_type=f32
        )
        out_ref[...] = (product * scale).astype(bf16)

    return call(
        kernel,
        "weight_products",
        (size // tile,),
        [*blocks, *grads],
        [columns(block, tile, start)] * count + [fixed(part.shape) for part in grads],
        [jax.ShapeDtypeStruct((features, width), bf16)],
        [pl.BlockSpec((tile, width), lambda i: (start + i, 0))],
        after,
        into,
        1024,
    )[0]


def last_step(slope, keep, far, into, offset, after):
    block, features = slope.shape
    size = keep.shape[1]
    tile = tile_of(offset, size, size)
    terms = list(far)

    def kernel(slope_ref, keep_ref, *refs):
        total = keep_ref[...]
        for ref in refs[:-1]:
            total = total + ref[...].astype(f32)
        refs[-1][...] = (total * slope_ref[...]).astype(bf16)

    return call(
        kernel,
        "last_step",
        (size // tile,),
        [slope, keep] + terms,
        [columns(block, tile, offset // tile)] + [columns(block, tile)] * (1 + len(terms)),
        [jax.ShapeDtypeStruct((block, features), bf16)],
        [columns(block, tile, offset // tile)],
        after,
        into,
        int(LAST_COST * 2**20 * size),
    )[0]


def solution(mesh):
    rows, cols, depths = mesh.shape["row"], mesh.shape["col"], mesh.shape["depth"]

    def per_device(preact, weight, out_grad):
        block, features = preact.shape
        row_tokens, width = out_grad.shape
        tokens = row_tokens * rows
        scale = 1.0 / math.sqrt(tokens)
        half = cols * block
        per_block = block // row_tokens
        ring = rows <= 4

        arrived = [from_next(preact, "col", cols, dx) for dx in range(1, cols)]
        parts = split_rows(out_grad, 2 if ring else 1, [])
        hidden = [hidden_part(preact, 0, features, [parts[0]])]
        slope = slopes(preact, [hidden[0]])

        if ring:
            pieces = [[part] for part in parts]
            for hop in range(rows - 1):
                for piece in pieces:
                    piece.append(to_next(piece[-1], "row", rows, 1))
        else:
            whole = lax.all_gather(parts[0], "row", axis=0, tiled=False)
            z = lax.axis_index("row")
            pieces = [
                [
                    lax.dynamic_index_in_dim(whole, lax.rem(z - s + rows, rows), 0, False)
                    for s in range(rows)
                ]
            ]

        def place_of(s):
            row = lax.rem(lax.axis_index("row") - s + rows, rows)
            owner = row // per_block
            dx = lax.rem(owner // depths - lax.axis_index("col") + cols, cols)
            dd = lax.rem(lax.rem(owner, depths) - lax.axis_index("depth") + depths, depths)
            return (dd * cols + dx) * per_block + lax.rem(row, per_block)

        hops = range(1, depths)
        early = staged(weight, cut(features, PARTIAL_CUTS)[0][1], [slope])
        first, second = in_order(pieces, place_of, half, tokens, [early])
        weights = [weight] + [from_next(weight, "depth", depths, dd) for dd in hops]
        grads = [first] + [
            to_next(second[(dd - 1) * half : dd * half], "depth", depths, dd) for dd in hops
        ]

        chunks = cut(features, PARTIAL_CUTS)
        count = len(chunks)
        owns, far = [], []
        for c, (offset, size) in enumerate(chunks):
            after = owns[-1:]
            own, send = partial_products(
                grads, weights, offset, size, block, after,
                early if c == 0 else None,
            )
            owns.append(own)
            far.append(
                [
                    to_next(send[(dx - 1) * block : dx * block], "col", cols, dx)
                    for dx in range(1, cols)
                ]
            )

        *raw, _ = lax.optimization_barrier((*arrived, owns[0]))
        blocks = hidden + raw
        blocks += [from_next(part, "depth", depths, dd) for dd in hops for part in blocks]
        weight_grad = None
        for k, (offset, size) in enumerate(cut(features, WEIGHT_CUTS)):
            after = owns[-1:] if k == 0 else far[k - 1][-1:]
            weight_grad = weight_products(
                blocks, cols, [first, second], weight_grad, offset, size, scale, after
            )
        preact_grad = None
        for c in range(count):
            preact_grad = last_step(
                slope, owns[c], far[c], preact_grad, chunks[c][0], [weight_grad] if c == 0 else []
            )
        return preact_grad, weight_grad

    return jax.shard_map(
        per_device,
        mesh=mesh,
        in_specs=(
            P(("group", "col", "depth"), "row"),
            P("row", ("col", "depth")),
            P(("group", "row"), ("col", "depth")),
        ),
        out_specs=(P(("group", "col", "depth"), "row"), P(("group", "row"), ("col", "depth"))),
        check_vma=False,
    )
```
